32 devices in a mesh: prime: 4 (over z), row: 8 (over y, x, core).
Axes of the slice: x: 2, y: 2, z: 4, core: 2. Of those that a mesh axis runs over, the one named last changes fastest.
Arguments:
- tile_data: bfloat16 [4, 32, 5, 128, 128], P('prime', 'row'), may hold values from -0.25 to 0.25
- tile_slots: int32 [4, 32, 5], P('prime', 'row'), may hold values from 0 to 19, as said below
- requests: int32 [4, 8, 8, 2], P('prime'), may hold values from 0 to 3, as said below
- start_panel: bfloat16 [4, 4096, 128], P('prime', 'row'), may hold values from -6 to 6
- projectors: bfloat16 [4, 4096, 128], P('prime', 'row'), may hold values from -0.125 to 0.125
- combine_weights: float32 [4, 4], replicated, may hold values from -3 to 3
Outputs:
- projections_mixed: float32 [4, 6, 128, 128], P(None, None, 'row', 'prime')
- final_panel: bfloat16 [4, 4096, 128], P('prime', 'row')
The draws below stay inside these ranges and needn't reach their ends.
Inputs may be any that keep to these rules, and one draw needn't show every extreme that they name: `tile_slots`: for each system and each device of row, the last slot of each of its 4 block rows is 16 plus the row's index among them, and the other slots of its rows together name each of 0 to 15 exactly once. `requests`: for each system, taking device and source device, the 2 entries are different.
All inputs are finite; a program needn't handle non-finite values.
Results may differ from the reference program's by a relative error of at most 0.02.
Values may be sent and summed in bfloat16 or wider, within the bound.
No kernel may reach another device: no remote copies, remote signals or barrier semaphores. Data moves between devices by JAX's collectives and lax.ppermute only.
A program may use at most 64 MiB of HBM per device.

```python
import jax
import jax.numpy as jnp
from jax import lax

TB = 128
W = 128
NB_DEV = 4
C = 2
ITERS = 6
PRIMES = 4
BLOCKS = 32
NQ = 4096
K = 5
N_ROW = 8


def draw_tile_slots(key, part):
    keys = jax.random.split(key, PRIMES * N_ROW)
    orders = jax.vmap(lambda single: jax.random.permutation(single, N_ROW * C))(keys)
    spread = orders.reshape(PRIMES, N_ROW, NB_DEV, N_ROW * C // NB_DEV).astype(jnp.int32)
    diagonal = N_ROW * C + jnp.arange(NB_DEV, dtype=jnp.int32)
    diagonal = jnp.broadcast_to(diagonal[None, None, :, None], (PRIMES, N_ROW, NB_DEV, 1))
    return jnp.concatenate([spread, diagonal], axis=3).reshape(PRIMES, BLOCKS, K).astype(jnp.int32)


def draw_requests(key, part):
    keys = jax.random.split(key, PRIMES * N_ROW * N_ROW)
    orders = jax.vmap(lambda single: jax.random.permutation(single, NB_DEV)[:C])(keys)
    return orders.reshape(PRIMES, N_ROW, N_ROW, C).astype(jnp.int32)


def raised(entries, stream_key, source, target, shards_of, factor):
    def block_of(position):
        return (jnp.arange(entries.shape[position]) // (entries.shape[position] // shards_of)).reshape((-1,) + (1,) * (entries.ndim - 1 - position))

    first = jax.random.permutation(stream_key, shards_of)[block_of(target)]
    other_side = (block_of(target) + shards_of // 2) % shards_of
    return jnp.where((block_of(source) == first) | (block_of(source) == other_side), factor * entries, entries)


def block_scale(rng, extent, shards, low, top_value):
    factor_of, own = 1.0, jax.random.fold_in(rng, 6)
    for axis_at, shards_of in shards:
        heights = jnp.exp(jax.random.uniform(jax.random.fold_in(own, axis_at), (shards_of,), jnp.float32, low / len(shards), top_value / len(shards)))
        factor_of = factor_of * jnp.repeat(heights, extent[axis_at] // shards_of).reshape([-1 if axis == axis_at else 1 for axis in range(len(extent))])
    return factor_of


def gaussian(key, extent, width, most, cuts=(), kind=jnp.bfloat16):
    entries = width * jax.random.normal(key, extent, jnp.float32)
    if cuts:
        entries = entries * block_scale(key, extent, cuts, -0.22, 0.18)
    return jnp.clip(entries, -most, most).astype(kind)


def bell_draw_with(rng, extent, width, bound, shards, heavy, held_as=jnp.bfloat16):
    array = width * jax.random.normal(rng, extent, jnp.float32)
    if shards:
        array = array * block_scale(rng, extent, shards, -0.22, 0.18)
    return jnp.clip(raised(array, jax.random.fold_in(rng, 3), *heavy), -bound, bound).astype(held_as)


def setup_inputs(seed: int = 0) -> dict:
    streams_of = jax.random.split(jax.random.key(seed), 7)
    return {
        "tile_data": gaussian(streams_of[0], (PRIMES, BLOCKS, K, TB, TB), (K * TB) ** -0.5, 0.25, ((0, 4), (1, 8))),
        "tile_slots": draw_tile_slots(jax.random.fold_in(streams_of[6], 71), 0),
        "requests": draw_requests(jax.random.fold_in(streams_of[6], 71), 0),
        "start_panel": gaussian(streams_of[3], (PRIMES, NQ, W), 1.0, 6.0, ((0, 4), (1, 8))),
        "projectors": bell_draw_with(streams_of[4], (PRIMES, NQ, W), NQ ** -0.5, 0.125, ((0, 4), (1, 8)), (1, 2, 8, 2.0)),
        "combine_weights": gaussian(streams_of[5], (PRIMES, PRIMES), PRIMES ** -0.5, 3.0, (), jnp.float32),
    }


def prime_columns(slot_table, wants):
    owner = (jnp.arange(BLOCKS, dtype=jnp.int32) // NB_DEV)[:, None]
    inside = jnp.clip(slot_table, 0, N_ROW * C - 1).astype(jnp.int32)
    source = inside // C
    within = inside % C
    picked = wants[owner, source, within]
    return jnp.where(slot_table < N_ROW * C, source * NB_DEV + picked, owner * NB_DEV + slot_table - N_ROW * C).astype(jnp.int32)


def one_prime(inputs):
    tiles_here, slots_here, wants_here, start_here, project_here = inputs
    columns = prime_columns(slots_here, wants_here)
    current = start_here
    term_list = []
    for iteration in range(ITERS):
        term_list.append(jnp.dot(project_here.T, current, preferred_element_type=jnp.float32))
        blocks = current.reshape(BLOCKS, TB, W)
        needed = blocks[columns].astype(jnp.float32)
        product = jnp.einsum('ikab,ikbw->iaw', tiles_here.astype(jnp.float32), needed)
        current = product.astype(jnp.bfloat16).reshape(NQ, W)
    return jnp.stack(term_list), current


def reference(tile_data, tile_slots, requests, start_panel, projectors, combine_weights):
    terms, final_panel = lax.map(one_prime, (tile_data, tile_slots, requests, start_panel, projectors))
    mixed = jnp.einsum('qp,pkab->qkab', combine_weights, terms, precision=lax.Precision.HIGHEST)
    return mixed, final_panel
```

```python
import functools

import jax
import jax.numpy as jnp
from jax import lax
from jax.experimental import pallas as pl
from jax.experimental.pallas import tpu as pltpu
from jax.sharding import PartitionSpec as P

ITERS = 6
WHOLE_BYTES = 12 << 20
VMEM_BYTES = 48 << 20


def bits_apart(ranks, distance):
    return [(rank, rank ^ distance) for rank in range(ranks)]


def column_order(shape, my_row, ranks, primes):
    width = shape[0]
    each = width // (ranks * primes)
    held = lax.broadcasted_iota(jnp.int32, shape, 0)
    column = lax.broadcasted_iota(jnp.int32, shape, 1)
    distance = lax.rem(column // each, ranks) ^ my_row
    place = distance * (primes * each) + column // (ranks * each) * each + lax.rem(column, each)
    return (held == place).astype(jnp.bfloat16)


def split_columns(ranks, primes, row_ref, panel_ref, *out_refs):
    rows, width = panel_ref.shape
    held = width // ranks
    order = column_order((width, width), row_ref[0], ranks, primes)
    turned = lax.dot_general(
        order, panel_ref[...], (((1,), (1,)), ((), ())), preferred_element_type=jnp.float32
    ).astype(jnp.bfloat16)
    size = out_refs[0].shape[3]
    for distance in range(ranks):
        for block in range(rows // size):
            out_refs[distance // 2][distance % 2, block] = turned[
                distance * held : (distance + 1) * held, block * size : (block + 1) * size
            ]


def apply_blocks(columns_ref, tile_refs, load, store):
    first = 0
    for tiles in tile_refs:
        blocks, stored, size, _ = tiles.shape
        for at in range(0, blocks, 2):
            panels, matrices = [], []
            for row in (at, at + 1):
                slots = [(first + row) * stored + k for k in range(stored)]
                panels.append(jnp.concatenate([load(columns_ref[s]) for s in slots], axis=1))
                matrices.append(jnp.concatenate([tiles[row, k] for k in range(stored)], axis=1))
            held = panels[0].shape[0]
            product = lax.dot_general(
                jnp.concatenate(panels, axis=0),
                jnp.concatenate(matrices, axis=0),
                (((1,), (1,)), ((), ())),
                preferred_element_type=jnp.float32,
            ).astype(jnp.bfloat16)
            store(first + at, product[:held, :size])
            store(first + at + 1, product[held:, size:])
        first += blocks


def first_steps(ranks, primes, columns_ref, *refs):
    chips = ranks // 2
    start_near, start_far = refs[:chips], refs[chips : 2 * chips]
    tiles = refs[2 * chips : 2 * chips + ranks]
    projectors = refs[2 * chips + ranks : 2 * chips + 2 * ranks]
    terms_ref, last_ref, history = refs[2 * chips + 2 * ranks :]
    _, blocks, held, size = start_near[0].shape
    for chip in range(chips):
        for block in range(blocks):
            history[2 * chip * blocks + block, :held] = start_near[chip][0, block]
            history[(2 * chip + 1) * blocks + block, :held] = start_far[chip][1, block]
    for step in range(ITERS - 1):
        old, new = slice(step * held, (step + 1) * held), slice((step + 1) * held, (step + 2) * held)

        def load(position):
            return history[position, old]

        def store(position, value):
            history[position, new] = value
            if step == ITERS - 2:
                last_ref[position] = value

        apply_blocks(columns_ref, tiles, load, store)
    total = None
    for rank in range(ranks):
        panels = jnp.concatenate([history[rank * blocks + b] for b in range(blocks)], axis=1)
        part = jnp.dot(panels, projectors[rank][...], preferred_element_type=jnp.float32)
        total = part if total is None else total + part
    each = held // primes
    for prime in range(primes):
        for step in range(ITERS):
            terms_ref[prime, step * each : (step + 1) * each] = total[
                step * held + prime * each : step * held + (prime + 1) * each
            ]


def last_step(columns_ref, panel_ref, *refs):
    tiles, out_ref = refs[:-1], refs[-1]

    def load(position):
        return panel_ref[position]

    def store(position, value):
        out_ref[position] = value

    apply_blocks(columns_ref, tiles, load, store)


def mix_terms(ranks, primes, place_ref, weights_ref, panel_ref, own_ref, *refs):
    others, out_refs = refs[: primes - 1], refs[primes - 1 : -1]
    turned = refs[-1]
    my_prime, my_row = place_ref[0], place_ref[1]
    parts = [own_ref[my_prime]] + [other[...] for other in others]
    rows, width = parts[0].shape
    mixed = []
    for prime in range(primes):
        mixed.append(sum(weights_ref[prime, my_prime ^ bits] * part for bits, part in enumerate(parts)))
    mixed.append(jnp.zeros((width - primes * rows, width), jnp.float32))
    turned[...] = jnp.concatenate(mixed, axis=0).T.astype(jnp.bfloat16).reshape(turned.shape)
    blocks = panel_ref.shape[0] // ranks
    held = panel_ref.shape[1]
    for distance in range(ranks):
        out = out_refs[distance // 2]
        for block in range(blocks):
            out[distance % 2, block * held : (block + 1) * held] = panel_ref[distance * blocks + block]
        out[distance % 2, blocks * held :] = turned[my_row ^ distance]


def join_columns(ranks, primes, row_ref, *refs):
    chips = ranks // 2
    near, far = refs[:chips], refs[chips : 2 * chips]
    mixed_ref, panel_ref = refs[2 * chips :]
    my_row = row_ref[0]
    width = panel_ref.shape[1]
    held = width // ranks
    each = held // primes
    order = column_order((width, width), my_row, ranks, primes)
    pieces = [(near, far)[d % 2][d // 2][d % 2] for d in range(ranks)]
    size = pieces[0].shape[1]
    blocks = panel_ref.shape[0] // size
    for block in range(blocks):
        turned = jnp.concatenate([p[block * held : (block + 1) * held] for p in pieces], axis=0)
        panel_ref[block * size : (block + 1) * size] = lax.dot_general(
            turned, order, (((0,), (0,)), ((), ())), preferred_element_type=jnp.float32
        ).astype(jnp.bfloat16)
    terms = jnp.concatenate([p[blocks * held :] for p in pieces], axis=1)
    part = ranks * each
    together = width // part
    shape = (ranks * width, width)
    source = lax.broadcasted_iota(jnp.int32, shape, 0)
    target = lax.broadcasted_iota(jnp.int32, shape, 1)
    distance = lax.rem(target // each, ranks) ^ my_row
    wanted = distance * width + target // part * each + lax.rem(target, each)
    for group in range(primes * ITERS // together):
        pick = (source == wanted + group * together * each).astype(jnp.bfloat16)
        placed = jnp.dot(terms, pick, preferred_element_type=jnp.float32)
        for at in range(together):
            entry = group * together + at
            mixed_ref[entry // ITERS, entry % ITERS] = placed[:, at * part : (at + 1) * part]


def on_chip(kernel, out_shape, smem, vmem, scratch=(), flops=0, name=None):
    space = [pl.BlockSpec(memory_space=pltpu.SMEM)] * len(smem) + [pl.BlockSpec(memory_space=pltpu.VMEM)] * len(vmem)
    return pl.pallas_call(
        kernel,
        out_shape=out_shape,
        in_specs=space,
        out_specs=jax.tree.map(lambda _: pl.BlockSpec(memory_space=pltpu.VMEM), out_shape),
        scratch_shapes=list(scratch),
        compiler_params=pltpu.CompilerParams(vmem_limit_bytes=VMEM_BYTES),
        cost_estimate=pl.CostEstimate(flops=flops, bytes_accessed=sum(v.size * v.dtype.itemsize for v in vmem), transcendentals=0),
        name=name,
    )(*smem, *vmem)


def own_columns(tile_slots, requests, my_row, ranks):
    blocks, stored = tile_slots.shape
    fetched = requests.shape[2]
    exchanged = ranks * fetched
    wants = lax.dynamic_index_in_dim(requests, my_row, 0, keepdims=False).reshape(exchanged)
    named = tile_slots[..., None] == lax.broadcasted_iota(jnp.int32, (1, 1, exchanged), 2)
    picked = jnp.sum(jnp.where(named, wants[None, None], 0), axis=2)
    return jnp.where(
        tile_slots < exchanged,
        tile_slots // fetched * blocks + picked,
        my_row * blocks + tile_slots - exchanged,
    )


def whole_system(tile_data, tile_slots, requests, start_panel, projectors, combine_weights):
    ranks, primes = lax.axis_size("row"), lax.axis_size("prime")
    chips = ranks // 2
    my_row, my_prime = lax.axis_index("row"), lax.axis_index("prime")
    row_word = my_row.reshape(1)
    tiles, panel, projector = tile_data[0], start_panel[0], projectors[0]
    blocks, stored, size, _ = tiles.shape
    width = panel.shape[1]
    held = width // ranks
    each = held // primes

    def from_chips(own):
        return [own] + [lax.ppermute(own, "row", bits_apart(ranks, 2 * chip)) for chip in range(1, chips)]

    def from_core(arrays):
        return [lax.ppermute(array, "row", bits_apart(ranks, 1)) for array in arrays]

    def by_distance(near, far):
        return [array for pair in zip(near, far) for array in pair]

    tiles_near = from_chips(tiles)
    tiles_far = from_core(tiles_near)
    pieces = on_chip(
        functools.partial(split_columns, ranks, primes),
        [jax.ShapeDtypeStruct((2, blocks, held, size), jnp.bfloat16)] * chips,
        [row_word],
        [panel],
        name="split_columns",
    )
    start_near = [pieces[0]] + [
        lax.ppermute(pieces[chip], "row", bits_apart(ranks, 2 * chip)) for chip in range(1, chips)
    ]
    start_far = from_core(start_near)
    columns = own_columns(tile_slots[0], requests[0], my_row, ranks)
    columns_near = jnp.stack(from_chips(columns))
    columns_far = lax.ppermute(columns_near, "row", bits_apart(ranks, 1))
    columns = jnp.stack([columns_near, columns_far], axis=1).reshape(-1)
    columns = (columns // blocks ^ my_row) * blocks + columns % blocks
    projectors_near = from_chips(projector)
    projectors_far = from_core(projectors_near)

    every_tile = by_distance(tiles_near, tiles_far)
    every_projector = by_distance(projectors_near, projectors_far)
    step_flops = 2 * ranks * tiles.size * held
    terms, panel = on_chip(
        functools.partial(first_steps, ranks, primes),
        [
            jax.ShapeDtypeStruct((primes, ITERS * each, width), jnp.float32),
            jax.ShapeDtypeStruct((ranks * blocks, held, size), jnp.bfloat16),
        ],
        [columns],
        [*start_near, *start_far, *every_tile, *every_projector],
        scratch=[pltpu.VMEM((ranks * blocks, ITERS * held, size), jnp.bfloat16)],
        flops=(ITERS - 1) * step_flops,
        name="first_steps",
    )
    others = [
        lax.ppermute(
            lax.dynamic_index_in_dim(terms, my_prime ^ bits, 0, keepdims=False), "prime", bits_apart(primes, bits)
        )
        for bits in range(1, primes)
    ]
    panel = on_chip(
        last_step,
        jax.ShapeDtypeStruct(panel.shape, jnp.bfloat16),
        [columns],
        [panel, *every_tile],
        flops=step_flops,
        name="last_step",
    )
    pieces = on_chip(
        functools.partial(mix_terms, ranks, primes),
        [jax.ShapeDtypeStruct((2, (blocks + 1) * held, size), jnp.bfloat16)] * chips,
        [jnp.stack([my_prime, my_row]), combine_weights],
        [panel, terms, *others],
        scratch=[pltpu.VMEM((ranks, width // ranks, width), jnp.bfloat16)],
        name="mix_terms",
    )
    near = [pieces[0]] + [lax.ppermute(pieces[chip], "row", bits_apart(ranks, 2 * chip)) for chip in range(1, chips)]
    far = from_core(near)
    mixed, panel = on_chip(
        functools.partial(join_columns, ranks, primes),
        [
            jax.ShapeDtypeStruct((primes, ITERS, width // ranks, width // primes), jnp.float32),
            jax.ShapeDtypeStruct((blocks * size, width), jnp.bfloat16),
        ],
        [row_word],
        [*near, *far],
        name="join_columns",
    )
    return mixed, panel[None]


def split_system(tile_data, tile_slots, requests, start_panel, projectors, combine_weights):
    ranks = lax.axis_size("row")
    my_row = lax.axis_index("row")
    blocks, stored, size, _ = tile_data.shape[1:]
    width = start_panel.shape[2]
    columns = own_columns(tile_slots[0], requests[0], my_row, ranks)
    panel, projector = start_panel[0], projectors[0]
    partial_sums = []
    for step in range(ITERS):
        partial_sums.append(
            jnp.dot(projector.T, panel, preferred_element_type=jnp.float32).astype(jnp.bfloat16)
        )
        gathered = lax.all_gather(panel, "row", axis=0, tiled=True)
        needed = gathered.reshape(ranks * blocks, size, width)[columns]
        product = jnp.einsum("ikab,ikbw->iaw", tile_data[0], needed, preferred_element_type=jnp.float32)
        panel = product.astype(jnp.bfloat16).reshape(blocks * size, width)
    terms = lax.psum_scatter(jnp.stack(partial_sums), "row", scatter_dimension=1, tiled=True).astype(jnp.float32)
    regrouped = lax.all_to_all(terms[None], "prime", split_axis=3, concat_axis=0, tiled=True)
    mixed = jnp.einsum("qp,pkab->qkab", combine_weights, regrouped, precision=lax.Precision.HIGHEST)
    return mixed, panel[None]


def shards(tile_data, *others):
    ranks, primes = lax.axis_size("row"), lax.axis_size("prime")
    whole_bytes = ranks * tile_data.size * tile_data.dtype.itemsize
    fits = whole_bytes <= WHOLE_BYTES and ranks == 8 and primes == 4 and tile_data.shape[3:] == (128, 128)
    return (whole_system if fits else split_system)(tile_data, *others)


def solution(mesh):
    return jax.shard_map(
        shards,
        mesh=mesh,
        in_specs=(
            P("prime", "row", None, None, None),
            P("prime", "row", None),
            P("prime", None, None, None),
            P("prime", "row", None),
            P("prime", "row", None),
            P(),
        ),
        out_specs=(P(None, None, "row", "prime"), P("prime", "row", None)),
        check_vma=False,
    )
```

```python
import functools

import jax
import jax.numpy as jnp
from jax import lax
from jax.experimental import pallas as pl
from jax.experimental.pallas import tpu as pltpu
from jax.sharding import PartitionSpec as P

ITERS = 6
WHOLE_BYTES = 12 << 20
VMEM_BYTES = 24 << 20


def bits_apart(ranks, distance):
    return [(rank, rank ^ distance) for rank in range(ranks)]


def pack_pieces(projectors_ref, columns_ref, out_ref):
    ranks = out_ref.shape[0]
    rows, width = projectors_ref.shape
    blocks, held = rows // width, width // ranks
    for block in range(blocks):
        turned = projectors_ref[block * width : (block + 1) * width].T
        for device in range(ranks):
            out_ref[device, block * held : (block + 1) * held] = turned[device * held : (device + 1) * held]
    for device in range(ranks):
        out_ref[device, blocks * held :] = columns_ref[...]


def cut_halves(first_ref, second_ref, after_ref, low_ref, high_ref):
    low_ref[...] = first_ref[: low_ref.shape[0]]
    high_ref[...] = second_ref[low_ref.shape[0] :]


def all_steps(ranks, primes, stored, columns_ref, place_ref, pieces_ref, *refs):
    refs, panels = refs[:-ITERS], refs[-ITERS:]
    refs, terms_refs, last_ref, terms = refs[: -primes - 2], refs[-primes - 2 : -2], refs[-2], refs[-1]
    middle = refs[-1].shape[0]
    refs = [whole.at[part] for whole in refs[:-4] for part in (slice(middle), slice(middle, 2 * middle))] + [*refs[-4:]]
    count, size, width = panels[0].shape
    blocks = count // ranks
    half = blocks // 2
    depth = half * stored * size
    first_of = [(place_ref[1] ^ distance) * blocks for distance in range(ranks)]
    for distance, first in enumerate(first_of):
        for row in range(blocks):
            source = refs[2 * distance + row // half]
            at = depth + row % half * size
            panels[0][first + row] = source[at : at + size]

    def apply_row(old, distance, row):
        source = refs[2 * distance + row // half]
        at = row % half * stored * size
        tiles = [source[at + k * size : at + (k + 1) * size] for k in range(stored)]
        slot = (first_of[distance] + row) * stored
        needed = [old[columns_ref[slot + k]] for k in range(stored)]
        return jnp.dot(
            jnp.concatenate(tiles, axis=1), jnp.concatenate(needed, axis=0), preferred_element_type=jnp.float32
        ).astype(jnp.bfloat16)

    for old, new in zip(panels[:-1], panels[1:]):
        for distance, first in enumerate(first_of):
            for row in range(blocks):
                new[first + row] = apply_row(old, distance, row)
    for row in range(blocks):
        last_ref[row * size : (row + 1) * size] = apply_row(panels[-1], 0, row)

    held = width // ranks
    parts = []
    for step in range(0, ITERS, 2):
        total = None
        for device in range(ranks):
            turned = [pieces_ref[device, block * held : (block + 1) * held] for block in range(blocks)]
            seen = [
                jnp.concatenate([panels[step + j][device * blocks + block] for j in range(2)], axis=1)
                for block in range(blocks)
            ]
            part = jnp.dot(
                jnp.concatenate(turned, axis=1), jnp.concatenate(seen, axis=0), preferred_element_type=jnp.float32
            )
            total = part if total is None else total + part
        parts += [total[:, :width], total[:, width:]]
    every_term = jnp.concatenate(parts, axis=0)
    rows, part = ITERS * held // primes, width // primes
    for prime in range(primes):
        terms[prime] = jnp.concatenate(
            [
                every_term[group * rows : (group + 1) * rows, prime * part : (prime + 1) * part]
                for group in range(primes)
            ],
            axis=1,
        )
    for bits in range(primes):
        terms_refs[bits][...] = terms[place_ref[0] ^ bits]


def mix_terms(place_ref, weights_ref, *refs):
    terms_refs, out_ref = refs[:-1], refs[-1]
    primes, steps, held, part = out_ref.shape
    parts = [terms[...] for terms in terms_refs]
    for prime in range(primes):
        mixed = sum(weights_ref[prime, place_ref[0] ^ bits] * terms for bits, terms in enumerate(parts))
        groups = [mixed[:, group * part : (group + 1) * part] for group in range(primes)]
        out_ref[prime] = jnp.concatenate(groups, axis=0).reshape(steps, held, part)


def on_chip(kernel, out_shape, smem, vmem, after=(), scratch=(), flops=0, name=None):
    spaces = [pltpu.SMEM] * len(smem) + [pltpu.VMEM] * len(vmem) + [pl.ANY] * len(after)
    return pl.pallas_call(
        kernel,
        out_shape=out_shape,
        in_specs=[pl.BlockSpec(memory_space=space) for space in spaces],
        out_specs=jax.tree.map(lambda _: pl.BlockSpec(memory_space=pltpu.VMEM), out_shape),
        scratch_shapes=list(scratch),
        compiler_params=pltpu.CompilerParams(vmem_limit_bytes=VMEM_BYTES),
        cost_estimate=pl.CostEstimate(flops=flops, bytes_accessed=sum(v.size * v.dtype.itemsize for v in vmem), transcendentals=0),
        name=name,
    )(*smem, *vmem, *after)


def own_columns(tile_slots, requests, my_row, ranks):
    blocks, stored = tile_slots.shape
    fetched = requests.shape[2]
    exchanged = ranks * fetched
    wants = lax.dynamic_index_in_dim(requests, my_row, 0, keepdims=False).reshape(exchanged)
    named = tile_slots[..., None] == lax.broadcasted_iota(jnp.int32, (1, 1, exchanged), 2)
    picked = jnp.sum(jnp.where(named, wants[None, None], 0), axis=2)
    return jnp.where(
        tile_slots < exchanged,
        tile_slots // fetched * blocks + picked,
        my_row * blocks + tile_slots - exchanged,
    )


def whole_system(tile_data, tile_slots, requests, start_panel, projectors, combine_weights):
    ranks, primes = lax.axis_size("row"), lax.axis_size("prime")
    my_row, my_prime = lax.axis_index("row"), lax.axis_index("prime")
    place = jnp.stack([my_prime, my_row])
    tiles, panel = tile_data[0], start_panel[0]
    blocks, stored, size, _ = tiles.shape
    width = panel.shape[1]
    held = width // ranks

    def to_chip(array, chip):
        return lax.ppermute(array, "row", bits_apart(ranks, 2 * chip))

    def to_core(array):
        return lax.ppermute(array, "row", bits_apart(ranks, 1))

    half = blocks // 2
    by_row = [tiles.reshape(blocks, stored * size, size), panel.reshape(blocks, size, width)]
    own = jnp.concatenate(
        [array[rows].reshape(-1, width) for rows in (slice(half), slice(half, blocks)) for array in by_row]
    )
    middle = own.shape[0] // 2
    from_x, from_y = to_chip(own, 1), to_chip(own, 2)
    columns = own_columns(tile_slots[0], requests[0], my_row, ranks)
    columns = jnp.pad(columns.astype(jnp.bfloat16), ((0, held - blocks), (0, width - stored)))
    pieces = on_chip(
        pack_pieces,
        jax.ShapeDtypeStruct((ranks, (blocks + 1) * held, width), jnp.bfloat16),
        [],
        [projectors[0], columns],
        name="pack_pieces",
    )
    pieces = lax.all_to_all(pieces, "row", split_axis=0, concat_axis=0, tiled=True)
    columns = pieces[:, blocks * held :][:, :blocks, :stored].astype(jnp.int32).reshape(-1)
    low, high = on_chip(
        cut_halves,
        [jax.ShapeDtypeStruct((middle, width), jnp.bfloat16)] * 2,
        [],
        [from_x, from_y],
        after=[pieces],
        name="cut_halves",
    )
    diagonal = [to_chip(low, 2), to_chip(high, 1)]
    whole = [array for near in (own, from_x, from_y) for array in (near, to_core(near))]
    halves = diagonal + [to_core(array) for array in diagonal]
    piece = jax.ShapeDtypeStruct((ITERS * held // primes, width), jnp.float32)
    *terms, last = on_chip(
        functools.partial(all_steps, ranks, primes, stored),
        [piece] * primes + [jax.ShapeDtypeStruct((blocks * size, width), jnp.bfloat16)],
        [columns, place],
        [pieces, *whole, *halves],
        scratch=[pltpu.VMEM((primes, *piece.shape), jnp.float32)]
        + [pltpu.VMEM((ranks * blocks, size, width), jnp.bfloat16)] * ITERS,
        flops=2 * ITERS * ranks * tiles.size * width,
        name="all_steps",
    )
    terms = [terms[0]] + [
        lax.ppermute(terms[bits], "prime", bits_apart(primes, bits)) for bits in range(1, primes)
    ]
    mixed = on_chip(
        mix_terms,
        jax.ShapeDtypeStruct((primes, ITERS, held, width // primes), jnp.float32),
        [place, combine_weights],
        terms,
        name="mix_terms",
    )
    return mixed, last[None]


def split_system(tile_data, tile_slots, requests, start_panel, projectors, combine_weights):
    ranks = lax.axis_size("row")
    my_row = lax.axis_index("row")
    blocks, stored, size, _ = tile_data.shape[1:]
    width = start_panel.shape[2]
    columns = own_columns(tile_slots[0], requests[0], my_row, ranks)
    panel, projector = start_panel[0], projectors[0]
    partial_sums = []
    for step in range(ITERS):
        partial_sums.append(
            jnp.dot(projector.T, panel, preferred_element_type=jnp.float32).astype(jnp.bfloat16)
        )
        gathered = lax.all_gather(panel, "row", axis=0, tiled=True)
        needed = gathered.reshape(ranks * blocks, size, width)[columns]
        product = jnp.einsum("ikab,ikbw->iaw", tile_data[0], needed, preferred_element_type=jnp.float32)
        panel = product.astype(jnp.bfloat16).reshape(blocks * size, width)
    terms = lax.psum_scatter(jnp.stack(partial_sums), "row", scatter_dimension=1, tiled=True).astype(jnp.float32)
    regrouped = lax.all_to_all(terms[None], "prime", split_axis=3, concat_axis=0, tiled=True)
    mixed = jnp.einsum("qp,pkab->qkab", combine_weights, regrouped, precision=lax.Precision.HIGHEST)
    return mixed, panel[None]


def shards(tile_data, *others):
    ranks, primes = lax.axis_size("row"), lax.axis_size("prime")
    whole_bytes = ranks * tile_data.size * tile_data.dtype.itemsize
    fits = whole_bytes <= WHOLE_BYTES and ranks == 8 and primes == 4 and tile_data.shape[3:] == (128, 128)
    return (whole_system if fits else split_system)(tile_data, *others)


def solution(mesh):
    return jax.shard_map(
        shards,
        mesh=mesh,
        in_specs=(
            P("prime", "row", None, None, None),
            P("prime", "row", None),
            P("prime", None, None, None),
            P("prime", "row", None),
            P("prime", "row", None),
            P(),
        ),
        out_specs=(P(None, None, "row", "prime"), P("prime", "row", None)),
        check_vma=False,
    )
```

```python
import functools

import jax
import jax.numpy as jnp
from jax import lax
from jax.experimental import pallas as pl
from jax.experimental.pallas import tpu as pltpu
from jax.sharding import PartitionSpec as P

ITERS = 6
WHOLE_BYTES = 12 << 20
VMEM_BYTES = 24 << 20


def bits_apart(ranks, distance):
    return [(rank, rank ^ distance) for rank in range(ranks)]


def pack_pieces(row_ref, panel_ref, projectors_ref, columns_ref, after_ref, *refs):
    out_refs, turned = refs[:-1], refs[-1]
    ranks, rows, width = turned.shape
    held = width // ranks
    blocks = rows // held
    for block in range(blocks):
        turned[:, block * held : (block + 1) * held] = projectors_ref[block * width : (block + 1) * width].T.reshape(
            ranks, held, width
        )
    first = panel_ref.shape[0]
    for chip, out in enumerate(out_refs):
        out[:first] = panel_ref[...]
        for core in range(2):
            at = first + core * rows
            out[at : at + rows] = turned[row_ref[0] ^ (2 * chip + core)]
        out[first + 2 * rows :] = columns_ref[...]


def cut_halves(first_ref, second_ref, same_first_ref, same_second_ref, low_ref, high_ref, arrived):
    rows = low_ref.shape[0]
    copies = [
        pltpu.make_async_copy(first_ref.at[:rows], low_ref, arrived.at[0]),
        pltpu.make_async_copy(second_ref.at[rows : 2 * rows], high_ref, arrived.at[1]),
    ]
    for copy in copies:
        copy.start()
    for copy in copies:
        copy.wait()


def join_pieces(*refs):
    pieces, out_ref = refs[:-2], refs[-1]
    rows = pieces[0].shape[0]
    for at, piece in enumerate(pieces):
        out_ref[at * rows : (at + 1) * rows] = piece[...]


def arrive(*refs):
    pass


def all_steps(ranks, primes, stored, columns_ref, place_ref, *refs):
    chips = ranks // 2
    near, joined, refs, panels = refs[:chips], refs[chips], refs[chips + 1 : -ITERS], refs[-ITERS:]
    refs, terms_refs, last_ref, terms = refs[: -primes - 2], refs[-primes - 2 : -2], refs[-2], refs[-1]
    count, size, width = panels[0].shape
    blocks = count // ranks
    half = blocks // 2
    rows, piece_rows = refs[-1].shape[0], near[0].shape[0]
    far = [joined.at[at * piece_rows : (at + 1) * piece_rows] for at in range(chips)]
    refs = [whole.at[at : at + rows] for whole in refs[:-4] for at in (0, rows)] + [*refs[-4:]]
    first_of = [(place_ref[1] ^ distance) * blocks for distance in range(ranks)]
    for distance, first in enumerate(first_of):
        piece = (near, far)[distance % 2][distance // 2]
        for row in range(blocks):
            panels[0][first + row] = piece[row * size : (row + 1) * size]

    def apply_row(old, distance, row):
        source = refs[2 * distance + row // half]
        at = row % half * stored * size
        tiles = [source[at + k * size : at + (k + 1) * size] for k in range(stored)]
        slot = (distance * blocks + row) * stored
        needed = [old[columns_ref[slot + k]] for k in range(stored)]
        return jnp.dot(
            jnp.concatenate(tiles, axis=1), jnp.concatenate(needed, axis=0), preferred_element_type=jnp.float32
        ).astype(jnp.bfloat16)

    for old, new in zip(panels[:-1], panels[1:]):
        for distance, first in enumerate(first_of):
            for row in range(blocks):
                new[first + row] = apply_row(old, distance, row)
    for row in range(blocks):
        last_ref[row * size : (row + 1) * size] = apply_row(panels[-1], 0, row)

    held = width // ranks
    parts = []
    for step in range(0, ITERS, 2):
        total = None
        for distance, first in enumerate(first_of):
            piece = (near, far)[distance % 2][distance // 2]
            at = blocks * size + distance % 2 * blocks * held
            turned = [piece[at + block * held : at + (block + 1) * held] for block in range(blocks)]
            seen = [
                jnp.concatenate([panels[step + j][first + block] for j in range(2)], axis=1) for block in range(blocks)
            ]
            part = jnp.dot(
                jnp.concatenate(turned, axis=1), jnp.concatenate(seen, axis=0), preferred_element_type=jnp.float32
            )
            total = part if total is None else total + part
        parts += [total[:, :width], total[:, width:]]
    every_term = jnp.concatenate(parts, axis=0)
    rows, part = ITERS * held // primes, width // primes
    for prime in range(primes):
        terms[prime] = jnp.concatenate(
            [
                every_term[group * rows : (group + 1) * rows, prime * part : (prime + 1) * part]
                for group in range(primes)
            ],
            axis=1,
        )
    for bits in range(primes):
        terms_refs[bits][...] = terms[place_ref[0] ^ bits]


def mix_terms(place_ref, weights_ref, *refs):
    terms_refs, out_ref = refs[:-1], refs[-1]
    primes, steps, held, part = out_ref.shape
    parts = [terms[...] for terms in terms_refs]
    for prime in range(primes):
        mixed = sum(weights_ref[prime, place_ref[0] ^ bits] * terms for bits, terms in enumerate(parts))
        groups = [mixed[:, group * part : (group + 1) * part] for group in range(primes)]
        out_ref[prime] = jnp.concatenate(groups, axis=0).reshape(steps, held, part)


def on_chip(kernel, out_shape, smem, vmem, before=(), after=(), aliases=None, scratch=(), flops=0, name=None):
    aliases = aliases or {}
    spaces = [pl.ANY] * len(before) + [pltpu.SMEM] * len(smem) + [pltpu.VMEM] * len(vmem) + [pl.ANY] * len(after)
    shapes, tree = jax.tree.flatten(out_shape)
    outs = [pl.BlockSpec(memory_space=pl.ANY if at in aliases.values() else pltpu.VMEM) for at in range(len(shapes))]
    return pl.pallas_call(
        kernel,
        out_shape=out_shape,
        in_specs=[pl.BlockSpec(memory_space=space) for space in spaces],
        out_specs=jax.tree.unflatten(tree, outs),
        scratch_shapes=list(scratch),
        input_output_aliases=aliases,
        compiler_params=pltpu.CompilerParams(vmem_limit_bytes=VMEM_BYTES),
        cost_estimate=pl.CostEstimate(flops=flops, bytes_accessed=sum(v.size * v.dtype.itemsize for v in vmem), transcendentals=0),
        name=name,
    )(*before, *smem, *vmem, *after)


def arrived(arrays, others):
    return on_chip(
        arrive,
        [jax.ShapeDtypeStruct(array.shape, array.dtype) for array in arrays],
        [],
        [],
        before=arrays,
        after=others,
        aliases={at: at for at in range(len(arrays))},
        flops=20_000_000_000,
        name="arrive",
    )


def own_columns(tile_slots, requests, my_row, ranks):
    blocks, stored = tile_slots.shape
    fetched = requests.shape[2]
    exchanged = ranks * fetched
    wants = lax.dynamic_index_in_dim(requests, my_row, 0, keepdims=False).reshape(exchanged)
    named = tile_slots[..., None] == lax.broadcasted_iota(jnp.int32, (1, 1, exchanged), 2)
    picked = jnp.sum(jnp.where(named, wants[None, None], 0), axis=2)
    return jnp.where(
        tile_slots < exchanged,
        tile_slots // fetched * blocks + picked,
        my_row * blocks + tile_slots - exchanged,
    )


def whole_system(tile_data, tile_slots, requests, start_panel, projectors, combine_weights):
    ranks, primes = lax.axis_size("row"), lax.axis_size("prime")
    my_row, my_prime = lax.axis_index("row"), lax.axis_index("prime")
    place = jnp.stack([my_prime, my_row])
    tiles, panel = tile_data[0], start_panel[0]
    blocks, stored, size, _ = tiles.shape
    width = panel.shape[1]
    held = width // ranks

    def to_chip(array, chip):
        return lax.ppermute(array, "row", bits_apart(ranks, 2 * chip))

    def to_core(array):
        return lax.ppermute(array, "row", bits_apart(ranks, 1))

    own = tiles.reshape(-1, width)
    from_x, from_y = to_chip(own, 1), to_chip(own, 2)
    own_far = to_core(own)
    columns = own_columns(tile_slots[0], requests[0], my_row, ranks)
    columns = jnp.pad(columns.astype(jnp.bfloat16), ((0, held - blocks), (0, width - stored)))
    chips = ranks // 2
    last_rows = blocks * size + 2 * blocks * held
    pieces = on_chip(
        pack_pieces,
        [jax.ShapeDtypeStruct((last_rows + held, width), jnp.bfloat16)] * chips,
        [my_row.reshape(1)],
        [panel, projectors[0], columns],
        after=[own_far],
        scratch=[pltpu.VMEM((ranks, blocks * held, width), jnp.bfloat16)],
        name="pack_pieces",
    )
    pieces = [pieces[0]] + [to_chip(pieces[chip], chip) for chip in range(1, chips)]
    half = jax.ShapeDtypeStruct((own.shape[0] // 2, width), jnp.bfloat16)
    whole = jax.ShapeDtypeStruct(own.shape, own.dtype)
    from_x, from_y, low, high = on_chip(
        cut_halves,
        [whole, whole, half, half],
        [],
        [],
        before=[from_x, from_y],
        aliases={0: 0, 1: 1},
        scratch=[pltpu.SemaphoreType.DMA((2,))],
        name="cut_halves",
    )
    diagonal = arrived([to_chip(low, 2), to_chip(high, 1)], [])
    joined = on_chip(
        join_pieces,
        jax.ShapeDtypeStruct((chips * pieces[0].shape[0], width), jnp.bfloat16),
        [],
        pieces,
        after=[low],
        name="join_pieces",
    )
    other = to_core(joined)
    columns = [piece[last_rows:][:blocks, :stored] for piece in pieces]
    other_columns = other.reshape(chips, -1, width)[:, last_rows:][:, :blocks, :stored]
    columns = jnp.stack([jnp.stack(columns), other_columns], axis=1).astype(jnp.int32).reshape(-1)
    whole = [own, own_far] + [array for near in (from_x, from_y) for array in (near, to_core(near))]
    halves = [*diagonal] + [to_core(array) for array in diagonal]
    piece = jax.ShapeDtypeStruct((ITERS * held // primes, width), jnp.float32)
    *terms, last = on_chip(
        functools.partial(all_steps, ranks, primes, stored),
        [piece] * primes + [jax.ShapeDtypeStruct((blocks * size, width), jnp.bfloat16)],
        [columns, place],
        [*pieces, other, *whole, *halves],
        scratch=[pltpu.VMEM((primes, *piece.shape), jnp.float32)]
        + [pltpu.VMEM((ranks * blocks, size, width), jnp.bfloat16)] * ITERS,
        flops=2 * ITERS * ranks * tiles.size * width,
        name="all_steps",
    )
    terms = [terms[0]] + [
        lax.ppermute(terms[bits], "prime", bits_apart(primes, bits)) for bits in range(1, primes)
    ]
    mixed = on_chip(
        mix_terms,
        jax.ShapeDtypeStruct((primes, ITERS, held, width // primes), jnp.float32),
        [place, combine_weights],
        terms,
        name="mix_terms",
    )
    return mixed, last[None]


def split_system(tile_data, tile_slots, requests, start_panel, projectors, combine_weights):
    ranks = lax.axis_size("row")
    my_row = lax.axis_index("row")
    blocks, stored, size, _ = tile_data.shape[1:]
    width = start_panel.shape[2]
    columns = own_columns(tile_slots[0], requests[0], my_row, ranks)
    panel, projector = start_panel[0], projectors[0]
    partial_sums = []
    for step in range(ITERS):
        partial_sums.append(
            jnp.dot(projector.T, panel, preferred_element_type=jnp.float32).astype(jnp.bfloat16)
        )
        gathered = lax.all_gather(panel, "row", axis=0, tiled=True)
        needed = gathered.reshape(ranks * blocks, size, width)[columns]
        product = jnp.einsum("ikab,ikbw->iaw", tile_data[0], needed, preferred_element_type=jnp.float32)
        panel = product.astype(jnp.bfloat16).reshape(blocks * size, width)
    terms = lax.psum_scatter(jnp.stack(partial_sums), "row", scatter_dimension=1, tiled=True).astype(jnp.float32)
    regrouped = lax.all_to_all(terms[None], "prime", split_axis=3, concat_axis=0, tiled=True)
    mixed = jnp.einsum("qp,pkab->qkab", combine_weights, regrouped, precision=lax.Precision.HIGHEST)
    return mixed, panel[None]


def shards(tile_data, *others):
    ranks, primes = lax.axis_size("row"), lax.axis_size("prime")
    whole_bytes = ranks * tile_data.size * tile_data.dtype.itemsize
    fits = whole_bytes <= WHOLE_BYTES and ranks == 8 and primes == 4 and tile_data.shape[3:] == (128, 128)
    return (whole_system if fits else split_system)(tile_data, *others)


def solution(mesh):
    return jax.shard_map(
        shards,
        mesh=mesh,
        in_specs=(
            P("prime", "row", None, None, None),
            P("prime", "row", None),
            P("prime", None, None, None),
            P("prime", "row", None),
            P("prime", "row", None),
            P(),
        ),
        out_specs=(P(None, None, "row", "prime"), P("prime", "row", None)),
        check_vma=False,
    )
```

```python
import functools

import jax
import jax.numpy as jnp
from jax import lax
from jax.experimental import pallas as pl
from jax.experimental.pallas import tpu as pltpu
from jax.sharding import PartitionSpec as P

ITERS = 6
WHOLE_BYTES = 12 << 20
VMEM_BYTES = 24 << 20


def bits_apart(ranks, distance):
    return [(rank, rank ^ distance) for rank in range(ranks)]


def pack_pieces(row_ref, panel_ref, projectors_ref, columns_ref, after_ref, *refs):
    out_refs, turned = refs[:-1], refs[-1]
    ranks, rows, width = turned.shape
    held = width // ranks
    blocks = rows // held
    for block in range(blocks):
        turned[:, block * held : (block + 1) * held] = projectors_ref[block * width : (block + 1) * width].T.reshape(
            ranks, held, width
        )
    first = panel_ref.shape[0]
    for chip, out in enumerate(out_refs):
        out[:first] = panel_ref[...]
        for core in range(2):
            at = first + core * rows
            out[at : at + rows] = turned[row_ref[0] ^ (2 * chip + core)]
        out[first + 2 * rows :] = columns_ref[...]


def cut_halves(first_ref, second_ref, after_ref, same_first_ref, same_second_ref, low_ref, high_ref, arrived):
    rows = low_ref.shape[0]
    copies = [
        pltpu.make_async_copy(first_ref.at[:rows], low_ref, arrived.at[0]),
        pltpu.make_async_copy(second_ref.at[rows : 2 * rows], high_ref, arrived.at[1]),
    ]
    for copy in copies:
        copy.start()
    for copy in copies:
        copy.wait()


def join_pieces(*refs):
    pieces, out_ref = refs[:-2], refs[-1]
    rows = pieces[0].shape[0]
    for at, piece in enumerate(pieces):
        out_ref[at * rows : (at + 1) * rows] = piece[...]


def arrive(*refs):
    pass


def apply_row(columns_ref, old, slot, stored, source, at):
    size = old.shape[1]
    tiles = [source[at + k * size : at + (k + 1) * size] for k in range(stored)]
    needed = [old[columns_ref[slot + k]] for k in range(stored)]
    return jnp.dot(
        jnp.concatenate(tiles, axis=1), jnp.concatenate(needed, axis=0), preferred_element_type=jnp.float32
    ).astype(jnp.bfloat16)


def first_step(ranks, stored, columns_ref, place_ref, *refs):
    chips = ranks // 2
    near, joined, tiles, (start_ref, part_ref, turned_ref) = refs[:chips], refs[chips], refs[chips + 1 : -3], refs[-3:]
    held_rows = turned_ref.shape[1]
    count, size, width = start_ref.shape
    blocks = count // ranks
    piece_rows = near[0].shape[0]
    for distance in range(ranks):
        first = (place_ref[1] ^ distance) * blocks
        piece = near[distance // 2]
        if distance % 2:
            piece = joined.at[distance // 2 * piece_rows : (distance // 2 + 1) * piece_rows]
        for row in range(blocks):
            start_ref[first + row] = piece[row * size : (row + 1) * size]
        at = blocks * size + distance % 2 * held_rows
        turned_ref[distance] = piece[at : at + held_rows]
    for row in range(part_ref.shape[0]):
        part_ref[row] = apply_row(
            columns_ref, start_ref, row * stored, stored, tiles[row // blocks], row % blocks * stored * size
        )


def all_steps(ranks, primes, stored, columns_ref, place_ref, *refs):
    (start, part, projectors), refs, panels = refs[:3], refs[3 : 1 - ITERS], refs[1 - ITERS :]
    refs, terms_refs, last_ref, terms = refs[: -primes - 2], refs[-primes - 2 : -2], refs[-2], refs[-1]
    count, size, width = start.shape
    blocks = count // ranks
    rows = refs[-1].shape[0]
    refs = [whole.at[at : at + rows] for whole in refs[:-4] for at in (0, rows)] + [*refs[-4:]]
    first_of = [(place_ref[1] ^ distance) * blocks for distance in range(ranks)]
    half = blocks // 2

    def apply(old, distance, row):
        return apply_row(
            columns_ref,
            old,
            (distance * blocks + row) * stored,
            stored,
            refs[2 * distance + row // half],
            row % half * stored * size,
        )

    panels = [start, *panels]
    for step, (old, new) in enumerate(zip(panels[:-1], panels[1:])):
        for distance, first in enumerate(first_of):
            for row in range(blocks):
                given = distance * blocks + row
                known = step == 0 and given < part.shape[0]
                new[first + row] = part[given] if known else apply(old, distance, row)
    for row in range(blocks):
        last_ref[row * size : (row + 1) * size] = apply(panels[-1], 0, row)

    held = width // ranks
    parts = []
    for step in range(0, ITERS, 2):
        total = None
        for distance, first in enumerate(first_of):
            turned = [projectors[distance, block * held : (block + 1) * held] for block in range(blocks)]
            seen = [
                jnp.concatenate([panels[step + j][first + block] for j in range(2)], axis=1) for block in range(blocks)
            ]
            part = jnp.dot(
                jnp.concatenate(turned, axis=1), jnp.concatenate(seen, axis=0), preferred_element_type=jnp.float32
            )
            total = part if total is None else total + part
        parts += [total[:, :width], total[:, width:]]
    every_term = jnp.concatenate(parts, axis=0)
    rows, part = ITERS * held // primes, width // primes
    for prime in range(primes):
        terms[prime] = jnp.concatenate(
            [
                every_term[group * rows : (group + 1) * rows, prime * part : (prime + 1) * part]
                for group in range(primes)
            ],
            axis=1,
        )
    for bits in range(primes):
        terms_refs[bits][...] = terms[place_ref[0] ^ bits]


def mix_terms(place_ref, weights_ref, *refs):
    terms_refs, out_ref = refs[:-1], refs[-1]
    primes, steps, held, part = out_ref.shape
    parts = [terms[...] for terms in terms_refs]
    for prime in range(primes):
        mixed = sum(weights_ref[prime, place_ref[0] ^ bits] * terms for bits, terms in enumerate(parts))
        groups = [mixed[:, group * part : (group + 1) * part] for group in range(primes)]
        out_ref[prime] = jnp.concatenate(groups, axis=0).reshape(steps, held, part)


def on_chip(kernel, out_shape, smem, vmem, before=(), after=(), aliases=None, scratch=(), flops=0, name=None):
    aliases = aliases or {}
    spaces = [pl.ANY] * len(before) + [pltpu.SMEM] * len(smem) + [pltpu.VMEM] * len(vmem) + [pl.ANY] * len(after)
    shapes, tree = jax.tree.flatten(out_shape)
    outs = [pl.BlockSpec(memory_space=pl.ANY if at in aliases.values() else pltpu.VMEM) for at in range(len(shapes))]
    return pl.pallas_call(
        kernel,
        out_shape=out_shape,
        in_specs=[pl.BlockSpec(memory_space=space) for space in spaces],
        out_specs=jax.tree.unflatten(tree, outs),
        scratch_shapes=list(scratch),
        input_output_aliases=aliases,
        compiler_params=pltpu.CompilerParams(vmem_limit_bytes=VMEM_BYTES),
        cost_estimate=pl.CostEstimate(flops=flops, bytes_accessed=sum(v.size * v.dtype.itemsize for v in vmem), transcendentals=0),
        name=name,
    )(*before, *smem, *vmem, *after)


def arrived(arrays, others):
    return on_chip(
        arrive,
        [jax.ShapeDtypeStruct(array.shape, array.dtype) for array in arrays],
        [],
        [],
        before=arrays,
        after=others,
        aliases={at: at for at in range(len(arrays))},
        flops=20_000_000_000,
        name="arrive",
    )


def own_columns(tile_slots, requests, my_row, ranks):
    blocks, stored = tile_slots.shape
    fetched = requests.shape[2]
    exchanged = ranks * fetched
    wants = lax.dynamic_index_in_dim(requests, my_row, 0, keepdims=False).reshape(exchanged)
    named = tile_slots[..., None] == lax.broadcasted_iota(jnp.int32, (1, 1, exchanged), 2)
    picked = jnp.sum(jnp.where(named, wants[None, None], 0), axis=2)
    return jnp.where(
        tile_slots < exchanged,
        tile_slots // fetched * blocks + picked,
        my_row * blocks + tile_slots - exchanged,
    )


def whole_system(tile_data, tile_slots, requests, start_panel, projectors, combine_weights):
    ranks, primes = lax.axis_size("row"), lax.axis_size("prime")
    my_row, my_prime = lax.axis_index("row"), lax.axis_index("prime")
    place = jnp.stack([my_prime, my_row])
    tiles, panel = tile_data[0], start_panel[0]
    blocks, stored, size, _ = tiles.shape
    width = panel.shape[1]
    held = width // ranks

    def to_chip(array, chip):
        return lax.ppermute(array, "row", bits_apart(ranks, 2 * chip))

    def to_core(array):
        return lax.ppermute(array, "row", bits_apart(ranks, 1))

    own = tiles.reshape(-1, width)
    from_x, from_y = to_chip(own, 1), to_chip(own, 2)
    own_far = to_core(own)
    columns = own_columns(tile_slots[0], requests[0], my_row, ranks)
    columns = jnp.pad(columns.astype(jnp.bfloat16), ((0, held - blocks), (0, width - stored)))
    chips = ranks // 2
    last_rows = blocks * size + 2 * blocks * held
    pieces = on_chip(
        pack_pieces,
        [jax.ShapeDtypeStruct((last_rows + held, width), jnp.bfloat16)] * chips,
        [my_row.reshape(1)],
        [panel, projectors[0], columns],
        after=[own_far],
        scratch=[pltpu.VMEM((ranks, blocks * held, width), jnp.bfloat16)],
        name="pack_pieces",
    )
    pieces = [pieces[0]] + [to_chip(pieces[chip], chip) for chip in range(1, chips)]
    half = jax.ShapeDtypeStruct((own.shape[0] // 2, width), jnp.bfloat16)
    whole = jax.ShapeDtypeStruct(own.shape, own.dtype)
    from_x, from_y, low, high = on_chip(
        cut_halves,
        [whole, whole, half, half],
        [],
        [],
        before=[from_x, from_y],
        after=pieces[:1],
        aliases={0: 0, 1: 1},
        scratch=[pltpu.SemaphoreType.DMA((2,))],
        name="cut_halves",
    )
    diagonal = [to_chip(low, 2), to_chip(high, 1)]
    joined = on_chip(
        join_pieces,
        jax.ShapeDtypeStruct((chips * pieces[0].shape[0], width), jnp.bfloat16),
        [],
        pieces,
        after=[low],
        name="join_pieces",
    )
    other = to_core(joined)
    columns = [piece[last_rows:][:blocks, :stored] for piece in pieces]
    other_columns = other.reshape(chips, -1, width)[:, last_rows:][:, :blocks, :stored]
    columns = jnp.stack([jnp.stack(columns), other_columns], axis=1).astype(jnp.int32).reshape(-1)
    whole = [own, own_far] + [array for near in (from_x, from_y) for array in (near, to_core(near))]
    piece = jax.ShapeDtypeStruct((ITERS * held // primes, width), jnp.float32)
    shape = (ranks * blocks, size, width)
    given = on_chip(
        functools.partial(first_step, ranks, stored),
        [
            jax.ShapeDtypeStruct(shape, jnp.bfloat16),
            jax.ShapeDtypeStruct(((ranks - 2) * blocks, size, width), jnp.bfloat16),
            jax.ShapeDtypeStruct((ranks, blocks * held, width), jnp.bfloat16),
        ],
        [columns, place],
        [*pieces, other, *whole],
        flops=2 * (ranks - 2) * tiles.size * width,
        name="first_step",
    )
    diagonal = arrived(diagonal, given[2:])
    halves = [*diagonal] + [to_core(array) for array in diagonal]
    *terms, last = on_chip(
        functools.partial(all_steps, ranks, primes, stored),
        [piece] * primes + [jax.ShapeDtypeStruct((blocks * size, width), jnp.bfloat16)],
        [columns, place],
        [*given, *whole, *halves],
        scratch=[pltpu.VMEM((primes, *piece.shape), jnp.float32)]
        + [pltpu.VMEM(shape, jnp.bfloat16)] * (ITERS - 1),
        flops=2 * ITERS * ranks * tiles.size * width,
        name="all_steps",
    )
    terms = [terms[0]] + [
        lax.ppermute(terms[bits], "prime", bits_apart(primes, bits)) for bits in range(1, primes)
    ]
    mixed = on_chip(
        mix_terms,
        jax.ShapeDtypeStruct((primes, ITERS, held, width // primes), jnp.float32),
        [place, combine_weights],
        terms,
        name="mix_terms",
    )
    return mixed, last[None]


def split_system(tile_data, tile_slots, requests, start_panel, projectors, combine_weights):
    ranks = lax.axis_size("row")
    my_row = lax.axis_index("row")
    blocks, stored, size, _ = tile_data.shape[1:]
    width = start_panel.shape[2]
    columns = own_columns(tile_slots[0], requests[0], my_row, ranks)
    panel, projector = start_panel[0], projectors[0]
    partial_sums = []
    for step in range(ITERS):
        partial_sums.append(
            jnp.dot(projector.T, panel, preferred_element_type=jnp.float32).astype(jnp.bfloat16)
        )
        gathered = lax.all_gather(panel, "row", axis=0, tiled=True)
        needed = gathered.reshape(ranks * blocks, size, width)[columns]
        product = jnp.einsum("ikab,ikbw->iaw", tile_data[0], needed, preferred_element_type=jnp.float32)
        panel = product.astype(jnp.bfloat16).reshape(blocks * size, width)
    terms = lax.psum_scatter(jnp.stack(partial_sums), "row", scatter_dimension=1, tiled=True).astype(jnp.float32)
    regrouped = lax.all_to_all(terms[None], "prime", split_axis=3, concat_axis=0, tiled=True)
    mixed = jnp.einsum("qp,pkab->qkab", combine_weights, regrouped, precision=lax.Precision.HIGHEST)
    return mixed, panel[None]


def shards(tile_data, *others):
    ranks, primes = lax.axis_size("row"), lax.axis_size("prime")
    whole_bytes = ranks * tile_data.size * tile_data.dtype.itemsize
    fits = whole_bytes <= WHOLE_BYTES and ranks == 8 and primes == 4 and tile_data.shape[3:] == (128, 128)
    return (whole_system if fits else split_system)(tile_data, *others)


def solution(mesh):
    return jax.shard_map(
        shards,
        mesh=mesh,
        in_specs=(
            P("prime", "row", None, None, None),
            P("prime", "row", None),
            P("prime", None, None, None),
            P("prime", "row", None),
            P("prime", "row", None),
            P(),
        ),
        out_specs=(P(None, None, "row", "prime"), P("prime", "row", None)),
        check_vma=False,
    )
```

```python
import functools

import jax
import jax.numpy as jnp
from jax import lax
from jax.experimental import pallas as pl
from jax.experimental.pallas import tpu as pltpu
from jax.sharding import PartitionSpec as P

ITERS = 6
WHOLE_BYTES = 12 << 20
VMEM_BYTES = 24 << 20


def bits_apart(ranks, distance):
    return [(rank, rank ^ distance) for rank in range(ranks)]


def pack_pieces(row_ref, panel_ref, projectors_ref, columns_ref, after_ref, *refs):
    out_refs, turned = refs[:-1], refs[-1]
    ranks, rows, width = turned.shape
    held = width // ranks
    blocks = rows // held
    for block in range(blocks):
        turned[:, block * held : (block + 1) * held] = projectors_ref[block * width : (block + 1) * width].T.reshape(
            ranks, held, width
        )
    first = panel_ref.shape[0]
    for chip, out in enumerate(out_refs):
        out[:first] = panel_ref[...]
        for core in range(2):
            at = first + core * rows
            out[at : at + rows] = turned[row_ref[0] ^ (2 * chip + core)]
        out[first + 2 * rows :] = columns_ref[...]


def cut_halves(first_ref, second_ref, after_ref, same_first_ref, same_second_ref, low_ref, high_ref, arrived):
    rows = low_ref.shape[0]
    copies = [
        pltpu.make_async_copy(first_ref.at[:rows], low_ref, arrived.at[0]),
        pltpu.make_async_copy(second_ref.at[rows : 2 * rows], high_ref, arrived.at[1]),
    ]
    for copy in copies:
        copy.start()
    for copy in copies:
        copy.wait()


def join_pieces(*refs):
    pieces, out_ref = refs[:-2], refs[-1]
    rows = pieces[0].shape[0]
    for at, piece in enumerate(pieces):
        out_ref[at * rows : (at + 1) * rows] = piece[...]


def arrive(*refs):
    pass


def apply_row(columns_ref, old, slot, stored, source, at):
    size = old.shape[1]
    tiles = [source[at + k * size : at + (k + 1) * size] for k in range(stored)]
    needed = [old[columns_ref[slot + k]] for k in range(stored)]
    return jnp.dot(
        jnp.concatenate(tiles, axis=1), jnp.concatenate(needed, axis=0), preferred_element_type=jnp.float32
    ).astype(jnp.bfloat16)


def first_step(ranks, stored, columns_ref, place_ref, *refs):
    chips = ranks // 2
    near, joined, tiles, (start_ref, part_ref, turned_ref) = refs[:chips], refs[chips], refs[chips + 1 : -3], refs[-3:]
    held_rows = turned_ref.shape[1]
    count, size, width = start_ref.shape
    blocks = count // ranks
    piece_rows = near[0].shape[0]
    for distance in range(ranks):
        first = (place_ref[1] ^ distance) * blocks
        piece = near[distance // 2]
        if distance % 2:
            piece = joined.at[distance // 2 * piece_rows : (distance // 2 + 1) * piece_rows]
        for row in range(blocks):
            start_ref[first + row] = piece[row * size : (row + 1) * size]
        at = blocks * size + distance % 2 * held_rows
        turned_ref[distance] = piece[at : at + held_rows]
    for row in range(part_ref.shape[0]):
        part_ref[row] = apply_row(
            columns_ref, start_ref, row * stored, stored, tiles[row // blocks], row % blocks * stored * size
        )


def all_steps(ranks, primes, stored, columns_ref, place_ref, *refs):
    (start, part, projectors), refs, panels = refs[:3], refs[3 : 1 - ITERS], refs[1 - ITERS :]
    refs, terms_refs, (last_ref, terms, result, sent) = refs[: -primes - 4], refs[-primes - 4 : -4], refs[-4:]
    count, size, width = start.shape
    blocks = count // ranks
    rows = refs[-1].shape[0]
    refs = [whole.at[at : at + rows] for whole in refs[:-4] for at in (0, rows)] + [*refs[-4:]]
    first_of = [(place_ref[1] ^ distance) * blocks for distance in range(ranks)]
    half = blocks // 2

    def apply(old, distance, row):
        return apply_row(
            columns_ref,
            old,
            (distance * blocks + row) * stored,
            stored,
            refs[2 * distance + row // half],
            row % half * stored * size,
        )

    panels = [start, *panels]
    for step, (old, new) in enumerate(zip(panels[:-1], panels[1:])):
        for distance, first in enumerate(first_of):
            for row in range(blocks):
                given = distance * blocks + row
                known = step == 0 and given < part.shape[0]
                new[first + row] = part[given] if known else apply(old, distance, row)
    for row in range(blocks):
        result[row * size : (row + 1) * size] = apply(panels[-1], 0, row)
    leaving = pltpu.make_async_copy(result, last_ref, sent.at[0])
    leaving.start()

    held = width // ranks
    parts = []
    for step in range(0, ITERS, 2):
        total = None
        for distance, first in enumerate(first_of):
            turned = [projectors[distance, block * held : (block + 1) * held] for block in range(blocks)]
            seen = [
                jnp.concatenate([panels[step + j][first + block] for j in range(2)], axis=1) for block in range(blocks)
            ]
            part = jnp.dot(
                jnp.concatenate(turned, axis=1), jnp.concatenate(seen, axis=0), preferred_element_type=jnp.float32
            )
            total = part if total is None else total + part
        parts += [total[:, :width], total[:, width:]]
    every_term = jnp.concatenate(parts, axis=0)
    rows, part = ITERS * held // primes, width // primes
    for prime in range(primes):
        terms[prime] = jnp.concatenate(
            [
                every_term[group * rows : (group + 1) * rows, prime * part : (prime + 1) * part]
                for group in range(primes)
            ],
            axis=1,
        )
    for bits in range(primes):
        terms_refs[bits][...] = terms[place_ref[0] ^ bits]
    leaving.wait()


def mix_terms(place_ref, weights_ref, *refs):
    terms_refs, out_ref = refs[:-1], refs[-1]
    primes, steps, held, part = out_ref.shape
    parts = [terms[...] for terms in terms_refs]
    for prime in range(primes):
        mixed = sum(weights_ref[prime, place_ref[0] ^ bits] * terms for bits, terms in enumerate(parts))
        groups = [mixed[:, group * part : (group + 1) * part] for group in range(primes)]
        out_ref[prime] = jnp.concatenate(groups, axis=0).reshape(steps, held, part)


def on_chip(kernel, out_shape, smem, vmem, before=(), after=(), aliases=None, far_outs=(), scratch=(), flops=0, name=None):
    aliases = aliases or {}
    spaces = [pl.ANY] * len(before) + [pltpu.SMEM] * len(smem) + [pltpu.VMEM] * len(vmem) + [pl.ANY] * len(after)
    shapes, tree = jax.tree.flatten(out_shape)
    far_outs = {*aliases.values(), *far_outs}
    outs = [pl.BlockSpec(memory_space=pl.ANY if at in far_outs else pltpu.VMEM) for at in range(len(shapes))]
    return pl.pallas_call(
        kernel,
        out_shape=out_shape,
        in_specs=[pl.BlockSpec(memory_space=space) for space in spaces],
        out_specs=jax.tree.unflatten(tree, outs),
        scratch_shapes=list(scratch),
        input_output_aliases=aliases,
        compiler_params=pltpu.CompilerParams(vmem_limit_bytes=VMEM_BYTES),
        cost_estimate=pl.CostEstimate(flops=flops, bytes_accessed=sum(v.size * v.dtype.itemsize for v in vmem), transcendentals=0),
        name=name,
    )(*before, *smem, *vmem, *after)


def arrived(arrays, others):
    return on_chip(
        arrive,
        [jax.ShapeDtypeStruct(array.shape, array.dtype) for array in arrays],
        [],
        [],
        before=arrays,
        after=others,
        aliases={at: at for at in range(len(arrays))},
        flops=20_000_000_000,
        name="arrive",
    )


def own_columns(tile_slots, requests, my_row, ranks):
    blocks, stored = tile_slots.shape
    fetched = requests.shape[2]
    exchanged = ranks * fetched
    wants = lax.dynamic_index_in_dim(requests, my_row, 0, keepdims=False).reshape(exchanged)
    named = tile_slots[..., None] == lax.broadcasted_iota(jnp.int32, (1, 1, exchanged), 2)
    picked = jnp.sum(jnp.where(named, wants[None, None], 0), axis=2)
    return jnp.where(
        tile_slots < exchanged,
        tile_slots // fetched * blocks + picked,
        my_row * blocks + tile_slots - exchanged,
    )


def whole_system(tile_data, tile_slots, requests, start_panel, projectors, combine_weights):
    ranks, primes = lax.axis_size("row"), lax.axis_size("prime")
    my_row, my_prime = lax.axis_index("row"), lax.axis_index("prime")
    place = jnp.stack([my_prime, my_row])
    tiles, panel = tile_data[0], start_panel[0]
    blocks, stored, size, _ = tiles.shape
    width = panel.shape[1]
    held = width // ranks

    def to_chip(array, chip):
        return lax.ppermute(array, "row", bits_apart(ranks, 2 * chip))

    def to_core(array):
        return lax.ppermute(array, "row", bits_apart(ranks, 1))

    own = tiles.reshape(-1, width)
    from_x, from_y = to_chip(own, 1), to_chip(own, 2)
    own_far = to_core(own)
    columns = own_columns(tile_slots[0], requests[0], my_row, ranks)
    columns = jnp.pad(columns.astype(jnp.bfloat16), ((0, held - blocks), (0, width - stored)))
    chips = ranks // 2
    last_rows = blocks * size + 2 * blocks * held
    pieces = on_chip(
        pack_pieces,
        [jax.ShapeDtypeStruct((last_rows + held, width), jnp.bfloat16)] * chips,
        [my_row.reshape(1)],
        [panel, projectors[0], columns],
        after=[own_far],
        scratch=[pltpu.VMEM((ranks, blocks * held, width), jnp.bfloat16)],
        name="pack_pieces",
    )
    pieces = [pieces[0]] + [to_chip(pieces[chip], chip) for chip in range(1, chips)]
    half = jax.ShapeDtypeStruct((own.shape[0] // 2, width), jnp.bfloat16)
    whole = jax.ShapeDtypeStruct(own.shape, own.dtype)
    from_x, from_y, low, high = on_chip(
        cut_halves,
        [whole, whole, half, half],
        [],
        [],
        before=[from_x, from_y],
        after=pieces[:1],
        aliases={0: 0, 1: 1},
        scratch=[pltpu.SemaphoreType.DMA((2,))],
        name="cut_halves",
    )
    diagonal = [to_chip(low, 2), to_chip(high, 1)]
    joined = on_chip(
        join_pieces,
        jax.ShapeDtypeStruct((chips * pieces[0].shape[0], width), jnp.bfloat16),
        [],
        pieces,
        after=[low],
        name="join_pieces",
    )
    other = to_core(joined)
    columns = [piece[last_rows:][:blocks, :stored] for piece in pieces]
    other_columns = other.reshape(chips, -1, width)[:, last_rows:][:, :blocks, :stored]
    columns = jnp.stack([jnp.stack(columns), other_columns], axis=1).astype(jnp.int32).reshape(-1)
    whole = [own, own_far] + [array for near in (from_x, from_y) for array in (near, to_core(near))]
    piece = jax.ShapeDtypeStruct((ITERS * held // primes, width), jnp.float32)
    shape = (ranks * blocks, size, width)
    given = on_chip(
        functools.partial(first_step, ranks, stored),
        [
            jax.ShapeDtypeStruct(shape, jnp.bfloat16),
            jax.ShapeDtypeStruct(((ranks - 2) * blocks, size, width), jnp.bfloat16),
            jax.ShapeDtypeStruct((ranks, blocks * held, width), jnp.bfloat16),
        ],
        [columns, place],
        [*pieces, other, *whole],
        flops=2 * (ranks - 2) * tiles.size * width,
        name="first_step",
    )
    diagonal = arrived(diagonal, given[2:])
    halves = [*diagonal] + [to_core(array) for array in diagonal]
    *terms, last = on_chip(
        functools.partial(all_steps, ranks, primes, stored),
        [piece] * primes + [jax.ShapeDtypeStruct((blocks * size, width), jnp.bfloat16)],
        [columns, place],
        [*given, *whole, *halves],
        far_outs=[primes],
        scratch=[
            pltpu.VMEM((primes, *piece.shape), jnp.float32),
            pltpu.VMEM((blocks * size, width), jnp.bfloat16),
            pltpu.SemaphoreType.DMA((1,)),
        ]
        + [pltpu.VMEM(shape, jnp.bfloat16)] * (ITERS - 1),
        flops=2 * ITERS * ranks * tiles.size * width,
        name="all_steps",
    )
    terms = [terms[0]] + [
        lax.ppermute(terms[bits], "prime", bits_apart(primes, bits)) for bits in range(1, primes)
    ]
    mixed = on_chip(
        mix_terms,
        jax.ShapeDtypeStruct((primes, ITERS, held, width // primes), jnp.float32),
        [place, combine_weights],
        terms,
        name="mix_terms",
    )
    return mixed, last[None]


def split_system(tile_data, tile_slots, requests, start_panel, projectors, combine_weights):
    ranks = lax.axis_size("row")
    my_row = lax.axis_index("row")
    blocks, stored, size, _ = tile_data.shape[1:]
    width = start_panel.shape[2]
    columns = own_columns(tile_slots[0], requests[0], my_row, ranks)
    panel, projector = start_panel[0], projectors[0]
    partial_sums = []
    for step in range(ITERS):
        partial_sums.append(
            jnp.dot(projector.T, panel, preferred_element_type=jnp.float32).astype(jnp.bfloat16)
        )
        gathered = lax.all_gather(panel, "row", axis=0, tiled=True)
        needed = gathered.reshape(ranks * blocks, size, width)[columns]
        product = jnp.einsum("ikab,ikbw->iaw", tile_data[0], needed, preferred_element_type=jnp.float32)
        panel = product.astype(jnp.bfloat16).reshape(blocks * size, width)
    terms = lax.psum_scatter(jnp.stack(partial_sums), "row", scatter_dimension=1, tiled=True).astype(jnp.float32)
    regrouped = lax.all_to_all(terms[None], "prime", split_axis=3, concat_axis=0, tiled=True)
    mixed = jnp.einsum("qp,pkab->qkab", combine_weights, regrouped, precision=lax.Precision.HIGHEST)
    return mixed, panel[None]


def shards(tile_data, *others):
    ranks, primes = lax.axis_size("row"), lax.axis_size("prime")
    whole_bytes = ranks * tile_data.size * tile_data.dtype.itemsize
    fits = whole_bytes <= WHOLE_BYTES and ranks == 8 and primes == 4 and tile_data.shape[3:] == (128, 128)
    return (whole_system if fits else split_system)(tile_data, *others)


def solution(mesh):
    return jax.shard_map(
        shards,
        mesh=mesh,
        in_specs=(
            P("prime", "row", None, None, None),
            P("prime", "row", None),
            P("prime", None, None, None),
            P("prime", "row", None),
            P("prime", "row", None),
            P(),
        ),
        out_specs=(P(None, None, "row", "prime"), P("prime", "row", None)),
        check_vma=False,
    )
```

```python
import functools

import jax
import jax.numpy as jnp
from jax import lax
from jax.experimental import pallas as pl
from jax.experimental.pallas import tpu as pltpu
from jax.sharding import PartitionSpec as P

ITERS = 6
WHOLE_BYTES = 12 << 20
VMEM_BYTES = 24 << 20


def bits_apart(ranks, distance):
    return [(rank, rank ^ distance) for rank in range(ranks)]


def pack_pieces(row_ref, panel_ref, projectors_ref, columns_ref, after_ref, *refs):
    out_refs, turned = refs[:-1], refs[-1]
    ranks, rows, width = turned.shape
    held = width // ranks
    blocks = rows // held
    for block in range(blocks):
        turned[:, block * held : (block + 1) * held] = projectors_ref[block * width : (block + 1) * width].T.reshape(
            ranks, held, width
        )
    first = panel_ref.shape[0]
    for chip, out in enumerate(out_refs):
        out[:first] = panel_ref[...]
        for core in range(2):
            at = first + core * rows
            out[at : at + rows] = turned[row_ref[0] ^ (2 * chip + core)]
        out[first + 2 * rows :] = columns_ref[...]


def cut_halves(first_ref, second_ref, after_ref, same_first_ref, same_second_ref, low_ref, high_ref, arrived):
    rows = low_ref.shape[0]
    copies = [
        pltpu.make_async_copy(first_ref.at[:rows], low_ref, arrived.at[0]),
        pltpu.make_async_copy(second_ref.at[rows : 2 * rows], high_ref, arrived.at[1]),
    ]
    for copy in copies:
        copy.start()
    for copy in copies:
        copy.wait()


def join_pieces(*refs):
    pieces, out_ref = refs[:-2], refs[-1]
    rows = pieces[0].shape[0]
    for at, piece in enumerate(pieces):
        out_ref[at * rows : (at + 1) * rows] = piece[...]


def arrive(*refs):
    pass


def apply_row(columns_ref, old, slot, stored, source, at):
    size = old.shape[1]
    tiles = [source[at + k * size : at + (k + 1) * size] for k in range(stored)]
    needed = [old[columns_ref[slot + k]] for k in range(stored)]
    return jnp.dot(
        jnp.concatenate(tiles, axis=1), jnp.concatenate(needed, axis=0), preferred_element_type=jnp.float32
    ).astype(jnp.bfloat16)


def first_step(ranks, stored, columns_ref, place_ref, *refs):
    chips = ranks // 2
    near, joined, tiles, (start_ref, part_ref, turned_ref) = refs[:chips], refs[chips], refs[chips + 1 : -3], refs[-3:]
    held_rows = turned_ref.shape[1]
    count, size, width = start_ref.shape
    blocks = count // ranks
    piece_rows = near[0].shape[0]
    for distance in range(ranks):
        first = (place_ref[1] ^ distance) * blocks
        piece = near[distance // 2]
        if distance % 2:
            piece = joined.at[distance // 2 * piece_rows : (distance // 2 + 1) * piece_rows]
        for row in range(blocks):
            start_ref[first + row] = piece[row * size : (row + 1) * size]
        at = blocks * size + distance % 2 * held_rows
        turned_ref[distance] = piece[at : at + held_rows]
    for row in range(part_ref.shape[0]):
        part_ref[row] = apply_row(
            columns_ref, start_ref, row * stored, stored, tiles[row // blocks], row % blocks * stored * size
        )


def all_steps(ranks, primes, stored, columns_ref, place_ref, *refs):
    (start, part, projectors), refs, panels = refs[:3], refs[3 : 1 - ITERS], refs[1 - ITERS :]
    refs, terms_refs, (last_ref, terms, result, sent) = refs[: -primes - 4], refs[-primes - 4 : -4], refs[-4:]
    count, size, width = start.shape
    blocks = count // ranks
    rows = refs[-1].shape[0]
    refs = [whole.at[at : at + rows] for whole in refs[:-4] for at in (0, rows)] + [*refs[-4:]]
    first_of = [(place_ref[1] ^ distance) * blocks for distance in range(ranks)]
    half = blocks // 2

    def apply(old, distance, row):
        return apply_row(
            columns_ref,
            old,
            (distance * blocks + row) * stored,
            stored,
            refs[2 * distance + row // half],
            row % half * stored * size,
        )

    panels = [start, *panels]
    for step, (old, new) in enumerate(zip(panels[:-1], panels[1:])):
        for distance, first in enumerate(first_of):
            for row in range(blocks):
                given = distance * blocks + row
                known = step == 0 and given < part.shape[0]
                new[first + row] = part[given] if known else apply(old, distance, row)
    for row in range(blocks):
        result[row * size : (row + 1) * size] = apply(panels[-1], 0, row)
    leaving = pltpu.make_async_copy(result, last_ref, sent.at[0])
    leaving.start()

    held = width // ranks
    parts = []
    for step in range(0, ITERS, 2):
        total = None
        for distance, first in enumerate(first_of):
            turned = [projectors[distance, block * held : (block + 1) * held] for block in range(blocks)]
            seen = [
                jnp.concatenate([panels[step + j][first + block] for j in range(2)], axis=1) for block in range(blocks)
            ]
            part = jnp.dot(
                jnp.concatenate(turned, axis=1), jnp.concatenate(seen, axis=0), preferred_element_type=jnp.float32
            )
            total = part if total is None else total + part
        parts += [total[:, :width], total[:, width:]]
    every_term = jnp.concatenate(parts, axis=0)
    rows, part = ITERS * held // primes, width // primes
    for prime in range(primes):
        terms[prime] = jnp.concatenate(
            [
                every_term[group * rows : (group + 1) * rows, prime * part : (prime + 1) * part]
                for group in range(primes)
            ],
            axis=1,
        )
    for bits in range(primes):
        terms_refs[bits][...] = terms[place_ref[0] ^ bits]
    leaving.wait()


def mix_terms(place_ref, weights_ref, *refs):
    terms_refs, (out_ref, mixture, sent) = refs[:-3], refs[-3:]
    primes, steps, held, part = mixture.shape
    copies = []
    parts = [terms[...] for terms in terms_refs]
    for prime in range(primes):
        mixed = sum(weights_ref[prime, place_ref[0] ^ bits] * terms for bits, terms in enumerate(parts))
        groups = [mixed[:, group * part : (group + 1) * part] for group in range(primes)]
        mixture[prime] = jnp.concatenate(groups, axis=0).reshape(steps, held, part)
        copies.append(pltpu.make_async_copy(mixture.at[prime], out_ref.at[prime], sent.at[prime]))
        copies[-1].start()
    for copy in copies:
        copy.wait()


def on_chip(kernel, out_shape, smem, vmem, before=(), after=(), aliases=None, far_outs=(), scratch=(), flops=0, name=None):
    aliases = aliases or {}
    spaces = [pl.ANY] * len(before) + [pltpu.SMEM] * len(smem) + [pltpu.VMEM] * len(vmem) + [pl.ANY] * len(after)
    shapes, tree = jax.tree.flatten(out_shape)
    far_outs = {*aliases.values(), *far_outs}
    outs = [pl.BlockSpec(memory_space=pl.ANY if at in far_outs else pltpu.VMEM) for at in range(len(shapes))]
    return pl.pallas_call(
        kernel,
        out_shape=out_shape,
        in_specs=[pl.BlockSpec(memory_space=space) for space in spaces],
        out_specs=jax.tree.unflatten(tree, outs),
        scratch_shapes=list(scratch),
        input_output_aliases=aliases,
        compiler_params=pltpu.CompilerParams(vmem_limit_bytes=VMEM_BYTES),
        cost_estimate=pl.CostEstimate(flops=flops, bytes_accessed=sum(v.size * v.dtype.itemsize for v in vmem), transcendentals=0),
        name=name,
    )(*before, *smem, *vmem, *after)


def arrived(arrays, others):
    return on_chip(
        arrive,
        [jax.ShapeDtypeStruct(array.shape, array.dtype) for array in arrays],
        [],
        [],
        before=arrays,
        after=others,
        aliases={at: at for at in range(len(arrays))},
        flops=20_000_000_000,
        name="arrive",
    )


def own_columns(tile_slots, requests, my_row, ranks):
    blocks, stored = tile_slots.shape
    fetched = requests.shape[2]
    exchanged = ranks * fetched
    wants = lax.dynamic_index_in_dim(requests, my_row, 0, keepdims=False).reshape(exchanged)
    named = tile_slots[..., None] == lax.broadcasted_iota(jnp.int32, (1, 1, exchanged), 2)
    picked = jnp.sum(jnp.where(named, wants[None, None], 0), axis=2)
    return jnp.where(
        tile_slots < exchanged,
        tile_slots // fetched * blocks + picked,
        my_row * blocks + tile_slots - exchanged,
    )


def whole_system(tile_data, tile_slots, requests, start_panel, projectors, combine_weights):
    ranks, primes = lax.axis_size("row"), lax.axis_size("prime")
    my_row, my_prime = lax.axis_index("row"), lax.axis_index("prime")
    place = jnp.stack([my_prime, my_row])
    tiles, panel = tile_data[0], start_panel[0]
    blocks, stored, size, _ = tiles.shape
    width = panel.shape[1]
    held = width // ranks

    def to_chip(array, chip):
        return lax.ppermute(array, "row", bits_apart(ranks, 2 * chip))

    def to_core(array):
        return lax.ppermute(array, "row", bits_apart(ranks, 1))

    own = tiles.reshape(-1, width)
    from_x, from_y = to_chip(own, 1), to_chip(own, 2)
    own_far = to_core(own)
    columns = own_columns(tile_slots[0], requests[0], my_row, ranks)
    columns = jnp.pad(columns.astype(jnp.bfloat16), ((0, held - blocks), (0, width - stored)))
    chips = ranks // 2
    last_rows = blocks * size + 2 * blocks * held
    pieces = on_chip(
        pack_pieces,
        [jax.ShapeDtypeStruct((last_rows + held, width), jnp.bfloat16)] * chips,
        [my_row.reshape(1)],
        [panel, projectors[0], columns],
        after=[own_far],
        scratch=[pltpu.VMEM((ranks, blocks * held, width), jnp.bfloat16)],
        name="pack_pieces",
    )
    pieces = [pieces[0]] + [to_chip(pieces[chip], chip) for chip in range(1, chips)]
    half = jax.ShapeDtypeStruct((own.shape[0] // 2, width), jnp.bfloat16)
    whole = jax.ShapeDtypeStruct(own.shape, own.dtype)
    from_x, from_y, low, high = on_chip(
        cut_halves,
        [whole, whole, half, half],
        [],
        [],
        before=[from_x, from_y],
        after=pieces[:1],
        aliases={0: 0, 1: 1},
        scratch=[pltpu.SemaphoreType.DMA((2,))],
        name="cut_halves",
    )
    diagonal = [to_chip(low, 2), to_chip(high, 1)]
    joined = on_chip(
        join_pieces,
        jax.ShapeDtypeStruct((chips * pieces[0].shape[0], width), jnp.bfloat16),
        [],
        pieces,
        after=[low],
        name="join_pieces",
    )
    other = to_core(joined)
    columns = [piece[last_rows:][:blocks, :stored] for piece in pieces]
    other_columns = other.reshape(chips, -1, width)[:, last_rows:][:, :blocks, :stored]
    columns = jnp.stack([jnp.stack(columns), other_columns], axis=1).astype(jnp.int32).reshape(-1)
    whole = [own, own_far] + [array for near in (from_x, from_y) for array in (near, to_core(near))]
    piece = jax.ShapeDtypeStruct((ITERS * held // primes, width), jnp.float32)
    shape = (ranks * blocks, size, width)
    given = on_chip(
        functools.partial(first_step, ranks, stored),
        [
            jax.ShapeDtypeStruct(shape, jnp.bfloat16),
            jax.ShapeDtypeStruct(((ranks - 2) * blocks, size, width), jnp.bfloat16),
            jax.ShapeDtypeStruct((ranks, blocks * held, width), jnp.bfloat16),
        ],
        [columns, place],
        [*pieces, other, *whole],
        flops=2 * (ranks - 2) * tiles.size * width,
        name="first_step",
    )
    diagonal = arrived(diagonal, given[2:])
    halves = [*diagonal] + [to_core(array) for array in diagonal]
    *terms, last = on_chip(
        functools.partial(all_steps, ranks, primes, stored),
        [piece] * primes + [jax.ShapeDtypeStruct((blocks * size, width), jnp.bfloat16)],
        [columns, place],
        [*given, *whole, *halves],
        far_outs=[primes],
        scratch=[
            pltpu.VMEM((primes, *piece.shape), jnp.float32),
            pltpu.VMEM((blocks * size, width), jnp.bfloat16),
            pltpu.SemaphoreType.DMA((1,)),
        ]
        + [pltpu.VMEM(shape, jnp.bfloat16)] * (ITERS - 1),
        flops=2 * ITERS * ranks * tiles.size * width,
        name="all_steps",
    )
    terms = [terms[0]] + [
        lax.ppermute(terms[bits], "prime", bits_apart(primes, bits)) for bits in range(1, primes)
    ]
    mixed = on_chip(
        mix_terms,
        jax.ShapeDtypeStruct((primes, ITERS, held, width // primes), jnp.float32),
        [place, combine_weights],
        terms,
        far_outs=[0],
        scratch=[
            pltpu.VMEM((primes, ITERS, held, width // primes), jnp.float32),
            pltpu.SemaphoreType.DMA((primes,)),
        ],
        name="mix_terms",
    )
    return mixed, last[None]


def split_system(tile_data, tile_slots, requests, start_panel, projectors, combine_weights):
    ranks = lax.axis_size("row")
    my_row = lax.axis_index("row")
    blocks, stored, size, _ = tile_data.shape[1:]
    width = start_panel.shape[2]
    columns = own_columns(tile_slots[0], requests[0], my_row, ranks)
    panel, projector = start_panel[0], projectors[0]
    partial_sums = []
    for step in range(ITERS):
        partial_sums.append(
            jnp.dot(projector.T, panel, preferred_element_type=jnp.float32).astype(jnp.bfloat16)
        )
        gathered = lax.all_gather(panel, "row", axis=0, tiled=True)
        needed = gathered.reshape(ranks * blocks, size, width)[columns]
        product = jnp.einsum("ikab,ikbw->iaw", tile_data[0], needed, preferred_element_type=jnp.float32)
        panel = product.astype(jnp.bfloat16).reshape(blocks * size, width)
    terms = lax.psum_scatter(jnp.stack(partial_sums), "row", scatter_dimension=1, tiled=True).astype(jnp.float32)
    regrouped = lax.all_to_all(terms[None], "prime", split_axis=3, concat_axis=0, tiled=True)
    mixed = jnp.einsum("qp,pkab->qkab", combine_weights, regrouped, precision=lax.Precision.HIGHEST)
    return mixed, panel[None]


def shards(tile_data, *others):
    ranks, primes = lax.axis_size("row"), lax.axis_size("prime")
    whole_bytes = ranks * tile_data.size * tile_data.dtype.itemsize
    fits = whole_bytes <= WHOLE_BYTES and ranks == 8 and primes == 4 and tile_data.shape[3:] == (128, 128)
    return (whole_system if fits else split_system)(tile_data, *others)


def solution(mesh):
    return jax.shard_map(
        shards,
        mesh=mesh,
        in_specs=(
            P("prime", "row", None, None, None),
            P("prime", "row", None),
            P("prime", None, None, None),
            P("prime", "row", None),
            P("prime", "row", None),
            P(),
        ),
        out_specs=(P(None, None, "row", "prime"), P("prime", "row", None)),
        check_vma=False,
    )
```
